256 devices in a mesh: gx: 4 (over y_lo, core), gy: 8 (over z), band: 8 (over y_hi, x).
Axes of the slice: x: 4, y: 4 (y_hi: 2, y_lo: 2; y = y_hi * 2 + y_lo), z: 8, core: 2. Of those that a mesh axis runs over, the one named last changes fastest.
Arguments:
- orbitals: bfloat16 [1152, 32, 16, 128], P('band', 'gx', 'gy'), may hold values from -6 to 6
- potential: float32 [32, 16, 128], P('gx', 'gy'), may hold values from -3 to 0.5
- panels: bfloat16 [2, 1152, 32, 16, 128], P(None, 'band', 'gx', 'gy'), may hold values from -6 to 6
Outputs:
- filtered: bfloat16 [1152, 32, 16, 128], P('band', 'gx', 'gy')
- margin: float32 [2, 1152, 1152], P(None, 'band', ('gx', 'gy'))
The draws below stay inside these ranges and needn't reach their ends.
All inputs are finite; a program needn't handle non-finite values.
Results may differ from the reference program's by a relative error of at most 0.0034.
Values may be sent and summed in bfloat16 or wider, within the bound.
A program may use at most 64 MiB of HBM per device.

```python
import math
import jax
import jax.numpy as jnp
from jax import lax

NB = 1152
PANELS = 2
NZ = 128
NX = 32
NY = 16


def steps_of(key, dims, split, low, largest):
    factor_of, own = 1.0, jax.random.fold_in(key, 6)
    for position, blocks in split:
        steps = jnp.exp(jax.random.uniform(jax.random.fold_in(own, position), (blocks,), jnp.float32, low / len(split), largest / len(split)))
        factor_of = factor_of * jnp.repeat(steps, dims[position] // blocks).reshape([-1 if axis == position else 1 for axis in range(len(dims))])
    return factor_of


def normal_values(own_key, shape, scale, most, split=(), dtype=jnp.bfloat16):
    drawn = scale * jax.random.normal(own_key, shape, jnp.float32)
    if split:
        drawn = drawn * steps_of(own_key, shape, split, -0.22, 0.18)
    return jnp.clip(drawn, -most, most).astype(dtype)


def setup_inputs(seed: int = 0) -> dict:
    key_of = jax.random.split(jax.random.key(seed), 4)
    orbitals = normal_values(key_of[0], (NB, NX, NY, NZ), 1.0, 6.0, ((0, 8), (1, 4), (2, 8)))
    potential = jnp.clip(-3.0 + 3.5 * jax.random.uniform(key_of[1], (NX, NY, NZ), jnp.float32) ** steps_of(key_of[1], (NX, NY, NZ), ((0, 4), (1, 8)), -0.2, 0.2), -3.0, 0.5)
    panels = normal_values(key_of[2], (PANELS, NB, NX, NY, NZ), 1.0, 6.0, ((1, 8), (2, 4), (3, 8)))
    return dict(orbitals=orbitals, potential=potential, panels=panels)


filter_center = 13.0
filter_half = 12.0

def hamiltonian(values, potential):
    neighbours = jnp.roll(values, -1, 1) + jnp.roll(values, 1, 1)
    neighbours = neighbours + jnp.roll(values, -1, 2) + jnp.roll(values, 1, 2)
    neighbours = neighbours + jnp.roll(values, -1, 3) + jnp.roll(values, 1, 3)
    return 2.0 * (6.0 * values - neighbours) + potential[None] * values

def reference(orbitals, potential, panels):

    def filter_block(source):
        values = source.astype(jnp.float32)
        first_section = ((hamiltonian(values, potential) - filter_center * values) / filter_half).astype(jnp.bfloat16)
        stored = first_section.astype(jnp.float32)
        return (2.0 * (hamiltonian(stored, potential) - filter_center * stored) / filter_half - values).astype(jnp.bfloat16)
    group = math.gcd(NB, 64)
    filtered = lax.map(filter_block, orbitals.reshape(NB // group, group, NX, NY, NZ)).reshape(NB, NX, NY, NZ)
    panel_rows = panels.reshape(PANELS * NB, NX * NY * NZ)
    flat = filtered.reshape(NB, NX * NY * NZ)
    product = lax.dot_general(panel_rows, flat, (((1,), (1,)), ((), ())), preferred_element_type=jnp.float32)
    margin = product.reshape(PANELS, NB, NB) * (1.0 / math.sqrt(NX * NY * NZ))
    return (filtered, margin)
```

```python
import functools
import math

import jax
import jax.numpy as jnp
from jax import lax
from jax.experimental import pallas as pl
from jax.experimental.pallas import tpu as pltpu
from jax.sharding import PartitionSpec as P

MESH = pl.DeviceIdType.MESH
NT = (((1,), (1,)), ((), ()))
CHUNKS = ((0, 48), (48, 64), (112, 32))


def kernel(
    scale,
    o_ref,
    pot_ref,
    p_ref,
    filt_ref,
    out_ref,
    potn,
    yb,
    xb,
    db,
    pan,
    first,
    fb,
    core_send,
    core_own,
    core_recv,
    y_send,
    y_recv,
    total,
    z_send,
    z_recv,
    halo_ss,
    halo_rs,
    pot_ss,
    pot_rs,
    pan_sem,
    own_sem,
    swap_ss,
    swap_rs,
    near_ss,
    near_rs,
    far_ss,
    far_rs,
    core_ss,
    core_rs,
    y_ss,
    y_rs,
    z_ss,
    z_rs,
):
    bf16, f32 = jnp.bfloat16, jnp.float32
    gx, gy, w = lax.axis_index("gx"), lax.axis_index("gy"), lax.axis_index("band")
    ylo, core = gx // 2, gx % 2
    yhi, xx = w // 4, w % 4
    ylo_other, core_other, yhi_other = 1 - ylo, 1 - core, 1 - yhi
    gx_prev, gx_next = (gx + 3) % 4, (gx + 1) % 4
    gy_prev, gy_next = (gy + 7) % 8, (gy + 1) % 8
    w_next, w_prev = yhi * 4 + (xx + 1) % 4, yhi * 4 + (xx + 3) % 4
    w_across = yhi_other * 4 + xx
    gx_core, gx_ylo = ylo * 2 + core_other, ylo_other * 2 + core

    barrier = pltpu.get_barrier_semaphore()
    partners = [(gx_prev, gy, w), (gx_next, gy, w)]
    partners += [(gx, (gy + d) % 8, w) for d in range(1, 8)]
    partners += [(a, b, w) for a in (gx_prev, gx_next) for b in (gy_prev, gy_next)]
    partners += [(gx, gy, w_across), (gx, gy, w_next), (gx, gy, w_prev)]
    partners += [(gx_ylo, gy, w), (gx_ylo, gy, w_across)]
    for device in partners:
        pl.semaphore_signal(barrier, 1, device_id=device, device_id_type=MESH)
    pl.semaphore_wait(barrier, len(partners))

    def remote(src, dst, ss, rs, device):
        return pltpu.make_async_remote_copy(
            src_ref=src, dst_ref=dst, send_sem=ss, recv_sem=rs, device_id=device, device_id_type=MESH
        )

    pending = []

    def start(copy):
        copy.start()
        pending.append(copy)
        return copy

    pots = [
        start(remote(pot_ref, potn.at[i], pot_ss.at[i], pot_rs.at[i], device))
        for i, device in enumerate(
            ((gx_next, gy, w), (gx_prev, gy, w), (gx, gy_next, w), (gx, gy_prev, w))
        )
    ]
    halos = []
    for k, (s0, n) in enumerate(CHUNKS):
        rows = pl.ds(s0, n)
        plan = (
            (o_ref.at[rows], yb.at[0, rows], (gx, gy_next, w)),
            (o_ref.at[rows], yb.at[1, rows], (gx, gy_prev, w)),
            (o_ref.at[rows, pl.ds(1536, 512)], xb.at[0, rows], (gx_next, gy, w)),
            (o_ref.at[rows, pl.ds(0, 512)], xb.at[1, rows], (gx_prev, gy, w)),
            (o_ref.at[rows, pl.ds(1920, 128)], db.at[0, rows], (gx_next, gy_next, w)),
            (o_ref.at[rows, pl.ds(1792, 128)], db.at[1, rows], (gx_next, gy_prev, w)),
            (o_ref.at[rows, pl.ds(128, 128)], db.at[2, rows], (gx_prev, gy_next, w)),
            (o_ref.at[rows, pl.ds(0, 128)], db.at[3, rows], (gx_prev, gy_prev, w)),
        )
        halos.append(
            [
                start(remote(src, dst, halo_ss.at[k, i], halo_rs.at[k, i], device))
                for i, (src, dst, device) in enumerate(plan)
            ]
        )
    mine, theirs = pl.ds(yhi * 1024, 1024), pl.ds(yhi_other * 1024, 1024)
    pan_own = pltpu.make_async_copy(p_ref.at[:, mine], pan.at[yhi], pan_sem.at[2])
    pan_own.start()
    pan_swap = start(
        remote(p_ref.at[:, theirs], pan.at[yhi], pan_sem.at[0], pan_sem.at[1], (gx, gy, w_across))
    )
    z_send[:, 32:48, :] = jnp.zeros((8, 16, z_send.shape[2]), bf16)

    def filter_rows(rows):
        def orb(x, y):
            if 0 <= x < 8:
                if y < 0:
                    piece = yb[0, rows, 128 * (2 * x + y + 2) : 128 * (2 * x + y + 3)]
                elif y > 1:
                    piece = yb[1, rows, 128 * (2 * x + y - 2) : 128 * (2 * x + y - 1)]
                else:
                    piece = o_ref[rows, 128 * (2 * x + y) : 128 * (2 * x + y + 1)]
            elif 0 <= y < 2:
                side, r = (0, 2 * (x + 2) + y) if x < 0 else (1, 2 * (x - 8) + y)
                piece = xb[side, rows, 128 * r : 128 * (r + 1)]
            else:
                piece = db[(0 if x < 0 else 2) + (0 if y < 0 else 1), rows, :]
            return piece.astype(f32)

        def slot(x, y):
            if 0 <= x < 8:
                return 2 * x + y if 0 <= y < 2 else (16 + x if y < 0 else 24 + x)
            return 32 + y if x < 0 else 34 + y

        def coefficient(x, y):
            if 0 <= x < 8 and 0 <= y < 2:
                p = pot_ref[2 * x + y : 2 * x + y + 1, :]
            elif y < 0:
                p = potn[2, 2 * x + 1 : 2 * x + 2, :]
            elif y > 1:
                p = potn[3, 2 * x : 2 * x + 1, :]
            elif x < 0:
                p = potn[0, 14 + y : 15 + y, :]
            else:
                p = potn[1, y : y + 1, :]
            return (p - 1.0) * (1.0 / 12.0)

        def both(v):
            return pltpu.roll(v, 1, 1) + pltpu.roll(v, 127, 1)

        cells = [(x, y) for x in range(8) for y in range(-1, 3)]
        cells += [(x, y) for x in (-1, 8) for y in (0, 1)]
        for x, y in cells:
            v = orb(x, y)
            s = orb(x + 1, y) + orb(x - 1, y) + orb(x, y + 1) + orb(x, y - 1) + both(v)
            first[slot(x, y)] = (coefficient(x, y) * v - s * (1.0 / 6.0)).astype(bf16).astype(f32)
        for x in range(8):
            for y in range(2):
                v = first[slot(x, y)]
                s = first[slot(x + 1, y)] + first[slot(x - 1, y)] + both(v)
                s = s + first[slot(x, y + 1)] + first[slot(x, y - 1)]
                value = 2.0 * coefficient(x, y) * v - s * (1.0 / 3.0) - orb(x, y)
                r = 2 * x + y
                filt_ref[rows, 128 * r : 128 * (r + 1)] = value.astype(bf16)

    swaps, owns, near, far = {}, {}, {}, {}
    cores, ys, zs = {}, {}, []

    def step_filter(k):
        s0, n = CHUNKS[k]
        if k == 0:
            for copy in pots:
                copy.wait_recv()
        for copy in halos[k]:
            copy.wait_recv()

        def sub(i, carry):
            filter_rows(pl.ds(pl.multiple_of(s0 + i * 16, 16), 16))
            return carry

        lax.fori_loop(0, n // 16, sub, 0)
        rows = pl.ds(s0, n)
        swaps[k] = start(
            remote(
                filt_ref.at[rows, theirs], fb.at[w, rows], swap_ss.at[k], swap_rs.at[k], (gx, gy, w_across)
            )
        )
        for d, to in enumerate((w_next, w_prev)):
            near[k, 0, d] = start(
                remote(
                    filt_ref.at[rows, mine],
                    fb.at[w, rows],
                    near_ss.at[k, 0, d],
                    near_rs.at[k, 0, d],
                    (gx, gy, to),
                )
            )
        owns[k] = pltpu.make_async_copy(filt_ref.at[rows, mine], fb.at[w, rows], own_sem.at[k])
        owns[k].start()

    def step_swap(k):
        s0, n = CHUNKS[k]
        rows = pl.ds(s0, n)
        swaps[k].wait_recv()
        for d, to in enumerate((w_next, w_prev)):
            near[k, 1, d] = start(
                remote(
                    fb.at[w_across, rows],
                    fb.at[w_across, rows],
                    near_ss.at[k, 1, d],
                    near_rs.at[k, 1, d],
                    (gx, gy, to),
                )
            )

    def step_forward(k, t):
        s0, n = CHUNKS[k]
        rows = pl.ds(s0, n)
        half = yhi if t == 0 else yhi_other
        for d, (to, origin) in enumerate(((w_next, (xx + 3) % 4), (w_prev, (xx + 1) % 4))):
            near[k, t, d].wait_recv()
            piece = fb.at[half * 4 + origin, rows, pl.ds(512 * d, 512)]
            far[k, t, d] = start(
                remote(piece, piece, far_ss.at[k, t, d], far_rs.at[k, t, d], (gx, gy, to))
            )

    def step_matmul(k):
        s0, n = CHUNKS[k]
        rows = pl.ds(s0, n)
        if k == 0:
            pan_own.wait()
            pan_swap.wait_recv()
        owns[k].wait()
        for t in range(2):
            for d in range(2):
                far[k, t, d].wait_recv()
        for side, dst in ((core_other, core_send), (core, core_own)):
            lhs = jnp.concatenate(
                [fb[4 * (q // 2) + 2 * side + q % 2, rows, :] for q in range(4)], axis=0
            )
            for rb in range(2):
                out = lax.dot_general(lhs, pan[rb], NT, preferred_element_type=f32) * scale
                for q in range(4):
                    dst[q // 2, q % 2, rb, rows, :] = out[n * q : n * (q + 1)]
            if dst is core_send:
                cores[k] = start(
                    remote(
                        core_send.at[:, :, :, rows],
                        core_recv.at[:, :, :, rows],
                        core_ss.at[k],
                        core_rs.at[k],
                        (gx_core, gy, w),
                    )
                )

    y_plan = (
        (ylo_other, yhi, (gx_ylo, gy, w)),
        (ylo, yhi_other, (gx, gy, w_across)),
        (ylo_other, yhi_other, (gx_ylo, gy, w_across)),
    )

    def step_core(k):
        s0, n = CHUNKS[k]
        rows = pl.ds(s0, n)
        cores[k].wait_recv()
        for j, (yl, yh, device) in enumerate(y_plan):
            for q in range(2):
                value = core_own[yl, q, yh, rows, :] + core_recv[yl, q, yh, rows, :]
                y_send[j, q, rows, :] = value.astype(bf16)
            ys[k, j] = start(
                remote(
                    y_send.at[j, :, rows], y_recv.at[j, :, rows], y_ss.at[k, j], y_rs.at[k, j], device
                )
            )
        for q in range(2):
            total[q, rows, :] = core_own[ylo, q, yhi, rows, :] + core_recv[ylo, q, yhi, rows, :]

    def step_y(k):
        s0, n = CHUNKS[k]
        rows = pl.ds(s0, n)
        for j in range(3):
            ys[k, j].wait_recv()
        for q in range(2):
            value = total[q, rows, :]
            for j in range(3):
                value = value + y_recv[j, q, rows, :].astype(f32)
            total[q, rows, :] = value
        done_before = s0 // 36
        for c in range(done_before, (s0 + n) // 36):
            for q in range(2):
                block = total[q, 36 * c : 36 * (c + 1), :]
                target = 4 * q + c

                @pl.when(target == gy)
                def _():
                    out_ref[0:36, :] = block

                @pl.when(target != gy)
                def _():
                    z_send[target, 0:36, :] = block.astype(bf16)
                    remote(
                        z_send.at[target], z_recv.at[gy], z_ss.at[target], z_rs.at[gy], (gx, target, w)
                    ).start()

    step_filter(0)
    step_swap(0)
    step_forward(0, 0)
    step_filter(1)
    step_forward(0, 1)
    step_swap(1)
    step_matmul(0)
    step_forward(1, 0)
    step_filter(2)
    step_forward(1, 1)
    step_swap(2)
    step_core(0)
    step_matmul(1)
    step_forward(2, 0)
    step_core(1)
    step_forward(2, 1)
    step_y(0)
    step_y(1)
    step_matmul(2)
    step_core(2)
    step_y(2)

    for s in range(8):

        @pl.when(s != gy)
        def _():
            copy = remote(z_send.at[s], z_recv.at[s], z_ss.at[s], z_rs.at[s], (gx, s, w))
            copy.wait_recv()
            out_ref[0:36, :] += z_recv[s, 0:36, :].astype(f32)
            copy.wait_send()

    for copy in pending:
        copy.wait_send()


def body(orbitals, potential, panels):
    bands, lx, ly, lz = orbitals.shape
    cells = lx * ly * lz
    panel_count = panels.shape[0]
    lines = panel_count * bands
    scale = 1.0 / math.sqrt(cells * lax.axis_size("gx") * lax.axis_size("gy"))
    bf16, f32 = jnp.bfloat16, jnp.float32
    c = len(CHUNKS)
    dma = pltpu.SemaphoreType.DMA
    filtered, sums = pl.pallas_call(
        functools.partial(kernel, scale),
        out_shape=(
            jax.ShapeDtypeStruct((bands, cells), bf16),
            jax.ShapeDtypeStruct((40, lines), f32),
        ),
        in_specs=[pl.BlockSpec(memory_space=pltpu.VMEM)] * 3,
        out_specs=(pl.BlockSpec(memory_space=pltpu.VMEM),) * 2,
        scratch_shapes=[
            pltpu.VMEM((4, lx * ly, lz), f32),
            pltpu.VMEM((2, bands, cells), bf16),
            pltpu.VMEM((2, bands, 512), bf16),
            pltpu.VMEM((4, bands, 128), bf16),
            pltpu.VMEM((2, lines, cells // 2), bf16),
            pltpu.VMEM((36, 16, 128), f32),
            pltpu.VMEM((8, bands, cells // 2), bf16),
            pltpu.VMEM((2, 2, 2, bands, lines), f32),
            pltpu.VMEM((2, 2, 2, bands, lines), f32),
            pltpu.VMEM((2, 2, 2, bands, lines), f32),
            pltpu.VMEM((3, 2, bands, lines), bf16),
            pltpu.VMEM((3, 2, bands, lines), bf16),
            pltpu.VMEM((2, bands, lines), f32),
            pltpu.VMEM((8, 48, lines), bf16),
            pltpu.VMEM((8, 48, lines), bf16),
            dma((c, 8)),
            dma((c, 8)),
            dma((4,)),
            dma((4,)),
            dma((3,)),
            dma((c,)),
            dma((c,)),
            dma((c,)),
            dma((c, 2, 2)),
            dma((c, 2, 2)),
            dma((c, 2, 2)),
            dma((c, 2, 2)),
            dma((c,)),
            dma((c,)),
            dma((c, 3)),
            dma((c, 3)),
            dma((8,)),
            dma((8,)),
        ],
        compiler_params=pltpu.CompilerParams(
            collective_id=0, has_side_effects=True, vmem_limit_bytes=48 << 20
        ),
        cost_estimate=pl.CostEstimate(
            flops=2 * lines * bands * 8 * cells, bytes_accessed=4 << 20, transcendentals=0
        ),
    )(
        orbitals.reshape(bands, cells),
        potential.reshape(lx * ly, lz),
        panels.reshape(lines, cells),
    )
    margin = sums[:36].T.reshape(panel_count, bands, 36)
    return filtered.reshape(orbitals.shape), margin


def solution(mesh):
    return jax.shard_map(
        body,
        mesh=mesh,
        in_specs=(
            P("band", "gx", "gy", None),
            P("gx", "gy", None),
            P(None, "band", "gx", "gy", None),
        ),
        out_specs=(P("band", "gx", "gy", None), P(None, "band", ("gx", "gy"))),
        check_vma=False,
    )
```

```python
import functools
import math

import jax
import jax.numpy as jnp
from jax import lax
from jax.experimental import pallas as pl
from jax.experimental.pallas import tpu as pltpu
from jax.sharding import PartitionSpec as P

MESH = pl.DeviceIdType.MESH
NT = (((1,), (1,)), ((), ()))
CHUNKS = ((0, 48), (48, 64), (112, 32))
PIECE = 48


def kernel(
    scale,
    o_ref,
    pot_ref,
    p_ref,
    filt_ref,
    out_ref,
    potn,
    yb,
    xb,
    db,
    pan,
    edge,
    lines_of,
    raw,
    side,
    result,
    first,
    mixed,
    fb,
    core_send,
    core_own,
    core_recv,
    y_send,
    y_recv,
    total,
    summed,
    z_send,
    z_recv,
    halo_ss,
    halo_rs,
    pot_ss,
    pot_rs,
    pan_sem,
    pan_ss,
    pan_rs,
    own_sem,
    swap_ss,
    swap_rs,
    near_ss,
    near_rs,
    far_ss,
    far_rs,
    core_ss,
    core_rs,
    y_ss,
    y_rs,
    z_ss,
    z_rs,
):
    bf16, f32 = jnp.bfloat16, jnp.float32
    gx, gy, w = lax.axis_index("gx"), lax.axis_index("gy"), lax.axis_index("band")
    ylo, core = gx // 2, gx % 2
    yhi, xx = w // 4, w % 4
    ylo_other, core_other, yhi_other = 1 - ylo, 1 - core, 1 - yhi
    gx_prev, gx_next = (gx + 3) % 4, (gx + 1) % 4
    gy_prev, gy_next = (gy + 7) % 8, (gy + 1) % 8
    w_next, w_prev = yhi * 4 + (xx + 1) % 4, yhi * 4 + (xx + 3) % 4
    w_across = yhi_other * 4 + xx
    gx_core, gx_ylo = ylo * 2 + core_other, ylo_other * 2 + core

    barrier = pltpu.get_barrier_semaphore()
    partners = [(gx_prev, gy, w), (gx_next, gy, w)]
    partners += [(gx, (gy + d) % 8, w) for d in range(1, 8)]
    partners += [(a, b, w) for a in (gx_prev, gx_next) for b in (gy_prev, gy_next)]
    partners += [(gx, gy, w_across), (gx, gy, w_next), (gx, gy, w_prev)]
    partners += [(gx_ylo, gy, w), (gx_ylo, gy, w_across)]
    for device in partners:
        pl.semaphore_signal(barrier, 1, device_id=device, device_id_type=MESH)

    def spread(src, dst, cell_rows, first_group, groups):
        def group(i, carry):
            raw[...] = src[pl.ds(pl.multiple_of(i * 256, 256), 256), :].astype(f32)
            rows = pl.ds(pl.multiple_of(i * 16, 16), 16)
            for j, r in enumerate(cell_rows):
                dst[rows, 128 * j : 128 * (j + 1)] = raw[pl.ds(r, 16, stride=16), :].astype(bf16)
            return carry

        lax.fori_loop(first_group, first_group + groups, group, 0)

    spread(o_ref, edge, (0, 1, 2, 3, 12, 13, 14, 15), 0, o_ref.shape[0] // 256)
    pl.semaphore_wait(barrier, len(partners))

    def remote(src, dst, ss, rs, device):
        return pltpu.make_async_remote_copy(
            src_ref=src, dst_ref=dst, send_sem=ss, recv_sem=rs, device_id=device, device_id_type=MESH
        )

    pending = []

    def start(copy):
        copy.start()
        pending.append(copy)
        return copy

    pots = [
        start(remote(pot_ref, potn.at[i], pot_ss.at[i], pot_rs.at[i], device))
        for i, device in enumerate(
            ((gx_next, gy, w), (gx_prev, gy, w), (gx, gy_next, w), (gx, gy_prev, w))
        )
    ]
    halos = {}

    def send_halo(k, places, plan):
        for i in places:
            src, dst, device = plan[i]
            halos[k, i] = start(remote(src, dst, halo_ss.at[k, i], halo_rs.at[k, i], device))

    def send_layers(k):
        s0, n = CHUNKS[k]
        rows = pl.ds(16 * s0, 16 * n)
        send_halo(
            k,
            (0, 1),
            (
                (o_ref.at[rows], yb.at[0, rows], (gx, gy_next, w)),
                (o_ref.at[rows], yb.at[1, rows], (gx, gy_prev, w)),
            ),
        )

    def send_edges(k):
        s0, n = CHUNKS[k]
        rows = pl.ds(s0, n)
        send_halo(
            k,
            range(2, 8),
            (
                None,
                None,
                (edge.at[rows, pl.ds(512, 512)], xb.at[0, rows], (gx_next, gy, w)),
                (edge.at[rows, pl.ds(0, 512)], xb.at[1, rows], (gx_prev, gy, w)),
                (edge.at[rows, pl.ds(896, 128)], db.at[0, rows], (gx_next, gy_next, w)),
                (edge.at[rows, pl.ds(768, 128)], db.at[1, rows], (gx_next, gy_prev, w)),
                (edge.at[rows, pl.ds(128, 128)], db.at[2, rows], (gx_prev, gy_next, w)),
                (edge.at[rows, pl.ds(0, 128)], db.at[3, rows], (gx_prev, gy_prev, w)),
            ),
        )

    send_layers(0)
    send_edges(0)
    for k in range(1, len(CHUNKS)):
        send_layers(k)
    mine, theirs = pl.ds(yhi * 1024, 1024), pl.ds(yhi_other * 1024, 1024)
    panel_swaps = []

    def swap_panels(count):
        for _ in range(count):
            i = len(panel_swaps)
            lines = pl.ds(i * PIECE, PIECE)
            spread(p_ref, lines_of, range(16), i * (PIECE // 16), PIECE // 16)
            panel_swaps.append(
                start(
                    remote(
                        lines_of.at[lines, theirs],
                        pan.at[yhi, lines],
                        pan_ss.at[i],
                        pan_rs.at[i],
                        (gx, gy, w_across),
                    )
                )
            )

    swap_panels(2)
    z_send[:, 32:48, :] = jnp.zeros((8, 16, z_send.shape[2]), bf16)

    def filter_rows(i):
        rows = pl.ds(pl.multiple_of(i * 16, 16), 16)
        stored = pl.ds(pl.multiple_of(i * 256, 256), 256)
        raw[...] = o_ref[stored, :].astype(f32)
        for d in range(2):
            side[d] = yb[d, stored, :].astype(f32)

        def orb(x, y):
            if 0 <= x < 8:
                if y < 0:
                    return side[0, pl.ds(2 * x + y + 2, 16, stride=16), :]
                if y > 1:
                    return side[1, pl.ds(2 * x + y - 2, 16, stride=16), :]
                return raw[pl.ds(2 * x + y, 16, stride=16), :]
            if 0 <= y < 2:
                d, r = (0, 2 * (x + 2) + y) if x < 0 else (1, 2 * (x - 8) + y)
                piece = xb[d, rows, 128 * r : 128 * (r + 1)]
            else:
                piece = db[(0 if x < 0 else 2) + (0 if y < 0 else 1), rows, :]
            return piece.astype(f32)

        def slot(x, y):
            if 0 <= x < 8:
                return 2 * x + y if 0 <= y < 2 else (16 + x if y < 0 else 24 + x)
            return 32 + y if x < 0 else 34 + y

        def coefficient(x, y):
            if 0 <= x < 8 and 0 <= y < 2:
                p = pot_ref[2 * x + y : 2 * x + y + 1, :]
            elif y < 0:
                p = potn[2, 2 * x + 1 : 2 * x + 2, :]
            elif y > 1:
                p = potn[3, 2 * x : 2 * x + 1, :]
            elif x < 0:
                p = potn[0, 14 + y : 15 + y, :]
            else:
                p = potn[1, y : y + 1, :]
            return (p - 1.0) * (1.0 / 12.0)

        def both(v):
            return pltpu.roll(v, 1, 1) + pltpu.roll(v, 127, 1)

        cells = [(x, y) for x in range(8) for y in range(-1, 3)]
        cells += [(x, y) for x in (-1, 8) for y in (0, 1)]
        for x, y in cells:
            v = orb(x, y)
            s = orb(x + 1, y) + orb(x - 1, y) + orb(x, y + 1) + orb(x, y - 1) + both(v)
            first[slot(x, y)] = (coefficient(x, y) * v - s * (1.0 / 6.0)).astype(bf16).astype(f32)
        for x in range(8):
            for y in range(2):
                v = first[slot(x, y)]
                s = first[slot(x + 1, y)] + first[slot(x - 1, y)] + both(v)
                s = s + first[slot(x, y + 1)] + first[slot(x, y - 1)]
                value = 2.0 * coefficient(x, y) * v - s * (1.0 / 3.0) - orb(x, y)
                r = 2 * x + y
                result[pl.ds(r, 16, stride=16), :] = value
                mixed[rows, 128 * r : 128 * (r + 1)] = value.astype(bf16)
        filt_ref[stored, :] = result[...].astype(bf16)

    swaps, owns, near, far = {}, {}, {}, {}
    cores, ys, zs = {}, {}, []

    def step_filter(k):
        s0, n = CHUNKS[k]
        if k == 0:
            for copy in pots:
                copy.wait_recv()
        for i in range(8):
            halos[k, i].wait_recv()

        def sub(i, carry):
            filter_rows(s0 // 16 + i)
            return carry

        lax.fori_loop(0, n // 16, sub, 0)
        rows = pl.ds(s0, n)
        swaps[k] = start(
            remote(
                mixed.at[rows, theirs], fb.at[w, rows], swap_ss.at[k], swap_rs.at[k], (gx, gy, w_across)
            )
        )
        for d, to in enumerate((w_next, w_prev)):
            near[k, 0, d] = start(
                remote(
                    mixed.at[rows, mine],
                    fb.at[w, rows],
                    near_ss.at[k, 0, d],
                    near_rs.at[k, 0, d],
                    (gx, gy, to),
                )
            )
        owns[k] = pltpu.make_async_copy(mixed.at[rows, mine], fb.at[w, rows], own_sem.at[k])
        owns[k].start()

    def step_swap(k):
        s0, n = CHUNKS[k]
        rows = pl.ds(s0, n)
        swaps[k].wait_recv()
        for d, to in enumerate((w_next, w_prev)):
            near[k, 1, d] = start(
                remote(
                    fb.at[w_across, rows],
                    fb.at[w_across, rows],
                    near_ss.at[k, 1, d],
                    near_rs.at[k, 1, d],
                    (gx, gy, to),
                )
            )

    def step_forward(k, t):
        s0, n = CHUNKS[k]
        rows = pl.ds(s0, n)
        half = yhi if t == 0 else yhi_other
        for d, (to, origin) in enumerate(((w_next, (xx + 3) % 4), (w_prev, (xx + 1) % 4))):
            near[k, t, d].wait_recv()
            piece = fb.at[half * 4 + origin, rows, pl.ds(512 * d, 512)]
            far[k, t, d] = start(
                remote(piece, piece, far_ss.at[k, t, d], far_rs.at[k, t, d], (gx, gy, to))
            )

    def step_matmul(k):
        s0, n = CHUNKS[k]
        rows = pl.ds(s0, n)
        if k == 0:
            pan_own = pltpu.make_async_copy(lines_of.at[:, mine], pan.at[yhi], pan_sem.at[0])
            pan_own.start()
            pan_own.wait()
            for copy in panel_swaps:
                copy.wait_recv()
        owns[k].wait()
        for t in range(2):
            for d in range(2):
                far[k, t, d].wait_recv()
        for side, dst in ((core_other, core_send), (core, core_own)):
            lhs = jnp.concatenate(
                [fb[4 * (q // 2) + 2 * side + q % 2, rows, :] for q in range(4)], axis=0
            )
            for rb in range(2):
                out = lax.dot_general(lhs, pan[rb], NT, preferred_element_type=f32) * scale
                for q in range(4):
                    dst[q // 2, q % 2, rb, rows, :] = out[n * q : n * (q + 1)]
            if dst is core_send:
                cores[k] = start(
                    remote(
                        core_send.at[:, :, :, rows],
                        core_recv.at[:, :, :, rows],
                        core_ss.at[k],
                        core_rs.at[k],
                        (gx_core, gy, w),
                    )
                )

    y_plan = (
        (ylo_other, yhi, (gx_ylo, gy, w)),
        (ylo, yhi_other, (gx, gy, w_across)),
        (ylo_other, yhi_other, (gx_ylo, gy, w_across)),
    )

    def step_core(k):
        s0, n = CHUNKS[k]
        rows = pl.ds(s0, n)
        cores[k].wait_recv()
        for j, (yl, yh, device) in enumerate(y_plan):
            for q in range(2):
                value = core_own[yl, q, yh, rows, :] + core_recv[yl, q, yh, rows, :]
                y_send[j, q, rows, :] = value.astype(bf16)
            ys[k, j] = start(
                remote(
                    y_send.at[j, :, rows], y_recv.at[j, :, rows], y_ss.at[k, j], y_rs.at[k, j], device
                )
            )
        for q in range(2):
            total[q, rows, :] = core_own[ylo, q, yhi, rows, :] + core_recv[ylo, q, yhi, rows, :]

    def step_y(k):
        s0, n = CHUNKS[k]
        rows = pl.ds(s0, n)
        for j in range(3):
            ys[k, j].wait_recv()
        for q in range(2):
            value = total[q, rows, :]
            for j in range(3):
                value = value + y_recv[j, q, rows, :].astype(f32)
            total[q, rows, :] = value
        done_before = s0 // 36
        for c in range(done_before, (s0 + n) // 36):
            for q in range(2):
                block = total[q, 36 * c : 36 * (c + 1), :]
                target = 4 * q + c

                @pl.when(target == gy)
                def _():
                    summed[0:36, :] = block

                @pl.when(target != gy)
                def _():
                    z_send[target, 0:36, :] = block.astype(bf16)
                    remote(
                        z_send.at[target], z_recv.at[gy], z_ss.at[target], z_rs.at[gy], (gx, target, w)
                    ).start()

    last = len(CHUNKS) - 1
    for k in range(last + 1):
        step_filter(k)
        if k < last:
            send_edges(k + 1)
        swap_panels((2, 2, 0)[k])
        if k > 0:
            step_forward(k - 1, 1)
        step_swap(k)
        if k < last:
            step_forward(k, 0)
    step_matmul(0)
    step_forward(last, 0)
    step_core(0)
    step_matmul(1)
    step_forward(last, 1)
    step_core(1)
    step_matmul(last)
    step_y(0)
    step_core(last)
    step_y(1)
    step_y(last)

    for s in range(8):

        @pl.when(s != gy)
        def _():
            copy = remote(z_send.at[s], z_recv.at[s], z_ss.at[s], z_rs.at[s], (gx, s, w))
            copy.wait_recv()
            summed[0:36, :] += z_recv[s, 0:36, :].astype(f32)
            copy.wait_send()

    lanes = out_ref.shape[2]
    for p in range(2):
        out_ref[:, p, :] = summed[0:36, lanes * p : lanes * (p + 1)]
    for copy in pending:
        copy.wait_send()


def body(orbitals, potential, panels):
    bands, lx, ly, lz = orbitals.shape
    cells = lx * ly * lz
    panel_count = panels.shape[0]
    lines = panel_count * bands
    scale = 1.0 / math.sqrt(cells * lax.axis_size("gx") * lax.axis_size("gy"))
    bf16, f32 = jnp.bfloat16, jnp.float32
    c = len(CHUNKS)
    dma = pltpu.SemaphoreType.DMA
    filtered, sums = pl.pallas_call(
        functools.partial(kernel, scale),
        out_shape=(
            jax.ShapeDtypeStruct((bands * lx * ly, lz), bf16),
            jax.ShapeDtypeStruct((36, panel_count, bands), f32),
        ),
        in_specs=[pl.BlockSpec(memory_space=pltpu.VMEM)] * 3,
        out_specs=(pl.BlockSpec(memory_space=pltpu.VMEM),) * 2,
        scratch_shapes=[
            pltpu.VMEM((4, lx * ly, lz), f32),
            pltpu.VMEM((2, bands * lx * ly, lz), bf16),
            pltpu.VMEM((2, bands, 512), bf16),
            pltpu.VMEM((4, bands, 128), bf16),
            pltpu.VMEM((2, lines, cells // 2), bf16),
            pltpu.VMEM((bands, 1024), bf16),
            pltpu.VMEM((lines, cells), bf16),
            pltpu.VMEM((256, lz), f32),
            pltpu.VMEM((2, 256, lz), f32),
            pltpu.VMEM((256, lz), f32),
            pltpu.VMEM((36, 16, 128), f32),
            pltpu.VMEM((bands, cells), bf16),
            pltpu.VMEM((8, bands, cells // 2), bf16),
            pltpu.VMEM((2, 2, 2, bands, lines), f32),
            pltpu.VMEM((2, 2, 2, bands, lines), f32),
            pltpu.VMEM((2, 2, 2, bands, lines), f32),
            pltpu.VMEM((3, 2, bands, lines), bf16),
            pltpu.VMEM((3, 2, bands, lines), bf16),
            pltpu.VMEM((2, bands, lines), f32),
            pltpu.VMEM((40, lines), f32),
            pltpu.VMEM((8, 48, lines), bf16),
            pltpu.VMEM((8, 48, lines), bf16),
            dma((c, 8)),
            dma((c, 8)),
            dma((4,)),
            dma((4,)),
            dma((1,)),
            dma((6,)),
            dma((6,)),
            dma((c,)),
            dma((c,)),
            dma((c,)),
            dma((c, 2, 2)),
            dma((c, 2, 2)),
            dma((c, 2, 2)),
            dma((c, 2, 2)),
            dma((c,)),
            dma((c,)),
            dma((c, 3)),
            dma((c, 3)),
            dma((8,)),
            dma((8,)),
        ],
        compiler_params=pltpu.CompilerParams(
            collective_id=0, has_side_effects=True, vmem_limit_bytes=48 << 20
        ),
        cost_estimate=pl.CostEstimate(
            flops=2 * lines * bands * 8 * cells, bytes_accessed=4 << 20, transcendentals=0
        ),
    )(
        orbitals.reshape(bands * lx * ly, lz),
        potential.reshape(lx * ly, lz),
        panels.reshape(lines * lx * ly, lz),
    )
    margin = sums.transpose(1, 2, 0)
    return filtered.reshape(orbitals.shape), margin


def solution(mesh):
    return jax.shard_map(
        body,
        mesh=mesh,
        in_specs=(
            P("band", "gx", "gy", None),
            P("gx", "gy", None),
            P(None, "band", "gx", "gy", None),
        ),
        out_specs=(P("band", "gx", "gy", None), P(None, "band", ("gx", "gy"))),
        check_vma=False,
    )
```

```python
import functools
import math

import jax
import jax.numpy as jnp
from jax import lax
from jax.experimental import pallas as pl
from jax.experimental.pallas import tpu as pltpu
from jax.sharding import PartitionSpec as P

MESH = pl.DeviceIdType.MESH
NT = (((1,), (1,)), ((), ()))
CHUNKS = ((0, 48), (48, 64), (112, 32))
PIECE = 48


def kernel(
    scale,
    o_ref,
    pot_ref,
    p_ref,
    filt_ref,
    out_ref,
    potn,
    yb,
    xb,
    db,
    pan,
    edge,
    lines_of,
    raw,
    side,
    result,
    first,
    mixed,
    fb,
    core_send,
    core_own,
    core_recv,
    y_send,
    y_recv,
    total,
    summed,
    z_send,
    z_recv,
    halo_ss,
    halo_rs,
    pot_ss,
    pot_rs,
    pan_sem,
    pan_ss,
    pan_rs,
    own_sem,
    swap_ss,
    swap_rs,
    near_ss,
    near_rs,
    far_ss,
    far_rs,
    core_ss,
    core_rs,
    y_ss,
    y_rs,
    z_ss,
    z_rs,
):
    bf16, f32 = jnp.bfloat16, jnp.float32
    gx, gy, w = lax.axis_index("gx"), lax.axis_index("gy"), lax.axis_index("band")
    ylo, core = gx // 2, gx % 2
    yhi, xx = w // 4, w % 4
    ylo_other, core_other = 1 - ylo, 1 - core
    half = (xx // 2 + xx) % 2
    half_other = 1 - half
    gx_prev, gx_next = (gx + 3) % 4, (gx + 1) % 4
    gy_prev, gy_next = (gy + 7) % 8, (gy + 1) % 8
    xx_across = xx + 1 - 2 * (xx % 2)
    w_across = yhi * 4 + xx_across
    w_near = ((1 - yhi) * 4 + xx, yhi * 4 + 3 - xx)
    w_near_across = ((1 - yhi) * 4 + xx_across, yhi * 4 + 3 - xx_across)
    gx_core, gx_ylo = ylo * 2 + core_other, ylo_other * 2 + core

    barrier = pltpu.get_barrier_semaphore()
    partners = [(gx_prev, gy, w), (gx_next, gy, w)]
    partners += [(gx, (gy + d) % 8, w) for d in range(1, 8)]
    partners += [(a, b, w) for a in (gx_prev, gx_next) for b in (gy_prev, gy_next)]
    partners += [(gx, gy, w_across), (gx, gy, w_near[0]), (gx, gy, w_near[1])]
    partners += [(gx_ylo, gy, w), (gx_ylo, gy, w_across)]
    for device in partners:
        pl.semaphore_signal(barrier, 1, device_id=device, device_id_type=MESH)

    def spread(src, dst, cell_rows, first_group, groups):
        def group(i, carry):
            raw[...] = src[pl.ds(pl.multiple_of(i * 256, 256), 256), :].astype(f32)
            rows = pl.ds(pl.multiple_of(i * 16, 16), 16)
            for j, r in enumerate(cell_rows):
                dst[rows, 128 * j : 128 * (j + 1)] = raw[pl.ds(r, 16, stride=16), :].astype(bf16)
            return carry

        lax.fori_loop(first_group, first_group + groups, group, 0)

    spread(o_ref, edge, (0, 1, 2, 3, 12, 13, 14, 15), 0, o_ref.shape[0] // 256)
    pl.semaphore_wait(barrier, len(partners))

    def remote(src, dst, ss, rs, device):
        return pltpu.make_async_remote_copy(
            src_ref=src, dst_ref=dst, send_sem=ss, recv_sem=rs, device_id=device, device_id_type=MESH
        )

    pending = []

    def start(copy):
        copy.start()
        pending.append(copy)
        return copy

    pots = [
        start(remote(pot_ref, potn.at[i], pot_ss.at[i], pot_rs.at[i], device))
        for i, device in enumerate(
            ((gx_next, gy, w), (gx_prev, gy, w), (gx, gy_next, w), (gx, gy_prev, w))
        )
    ]
    halos = {}

    def send_halo(k, places, plan):
        for i in places:
            src, dst, device = plan[i]
            halos[k, i] = start(remote(src, dst, halo_ss.at[k, i], halo_rs.at[k, i], device))

    def send_layers(k):
        s0, n = CHUNKS[k]
        rows = pl.ds(16 * s0, 16 * n)
        send_halo(
            k,
            (0, 1),
            (
                (o_ref.at[rows], yb.at[0, rows], (gx, gy_next, w)),
                (o_ref.at[rows], yb.at[1, rows], (gx, gy_prev, w)),
            ),
        )

    def send_edges(k):
        s0, n = CHUNKS[k]
        rows = pl.ds(s0, n)
        send_halo(
            k,
            range(2, 8),
            (
                None,
                None,
                (edge.at[rows, pl.ds(512, 512)], xb.at[0, rows], (gx_next, gy, w)),
                (edge.at[rows, pl.ds(0, 512)], xb.at[1, rows], (gx_prev, gy, w)),
                (edge.at[rows, pl.ds(896, 128)], db.at[0, rows], (gx_next, gy_next, w)),
                (edge.at[rows, pl.ds(768, 128)], db.at[1, rows], (gx_next, gy_prev, w)),
                (edge.at[rows, pl.ds(128, 128)], db.at[2, rows], (gx_prev, gy_next, w)),
                (edge.at[rows, pl.ds(0, 128)], db.at[3, rows], (gx_prev, gy_prev, w)),
            ),
        )

    send_layers(0)
    send_edges(0)
    for k in range(1, len(CHUNKS)):
        send_layers(k)
    mine, theirs = pl.ds(half * 1024, 1024), pl.ds(half_other * 1024, 1024)
    panel_swaps = []

    def swap_panels(count):
        for _ in range(count):
            i = len(panel_swaps)
            lines = pl.ds(i * PIECE, PIECE)
            spread(p_ref, lines_of, range(16), i * (PIECE // 16), PIECE // 16)
            panel_swaps.append(
                start(
                    remote(
                        lines_of.at[lines, theirs],
                        pan.at[half, lines],
                        pan_ss.at[i],
                        pan_rs.at[i],
                        (gx, gy, w_across),
                    )
                )
            )

    swap_panels(2)
    z_send[:, 32:48, :] = jnp.zeros((8, 16, z_send.shape[2]), bf16)

    def filter_rows(i):
        rows = pl.ds(pl.multiple_of(i * 16, 16), 16)
        stored = pl.ds(pl.multiple_of(i * 256, 256), 256)
        raw[...] = o_ref[stored, :].astype(f32)
        for d in range(2):
            side[d] = yb[d, stored, :].astype(f32)

        def orb(x, y):
            if 0 <= x < 8:
                if y < 0:
                    return side[0, pl.ds(2 * x + y + 2, 16, stride=16), :]
                if y > 1:
                    return side[1, pl.ds(2 * x + y - 2, 16, stride=16), :]
                return raw[pl.ds(2 * x + y, 16, stride=16), :]
            if 0 <= y < 2:
                d, r = (0, 2 * (x + 2) + y) if x < 0 else (1, 2 * (x - 8) + y)
                piece = xb[d, rows, 128 * r : 128 * (r + 1)]
            else:
                piece = db[(0 if x < 0 else 2) + (0 if y < 0 else 1), rows, :]
            return piece.astype(f32)

        def slot(x, y):
            if 0 <= x < 8:
                return 2 * x + y if 0 <= y < 2 else (16 + x if y < 0 else 24 + x)
            return 32 + y if x < 0 else 34 + y

        def coefficient(x, y):
            if 0 <= x < 8 and 0 <= y < 2:
                p = pot_ref[2 * x + y : 2 * x + y + 1, :]
            elif y < 0:
                p = potn[2, 2 * x + 1 : 2 * x + 2, :]
            elif y > 1:
                p = potn[3, 2 * x : 2 * x + 1, :]
            elif x < 0:
                p = potn[0, 14 + y : 15 + y, :]
            else:
                p = potn[1, y : y + 1, :]
            return (p - 1.0) * (1.0 / 12.0)

        def both(v):
            return pltpu.roll(v, 1, 1) + pltpu.roll(v, 127, 1)

        cells = [(x, y) for x in range(8) for y in range(-1, 3)]
        cells += [(x, y) for x in (-1, 8) for y in (0, 1)]
        for x, y in cells:
            v = orb(x, y)
            s = orb(x + 1, y) + orb(x - 1, y) + orb(x, y + 1) + orb(x, y - 1) + both(v)
            first[slot(x, y)] = (coefficient(x, y) * v - s * (1.0 / 6.0)).astype(bf16).astype(f32)
        for x in range(8):
            for y in range(2):
                v = first[slot(x, y)]
                s = first[slot(x + 1, y)] + first[slot(x - 1, y)] + both(v)
                s = s + first[slot(x, y + 1)] + first[slot(x, y - 1)]
                value = 2.0 * coefficient(x, y) * v - s * (1.0 / 3.0) - orb(x, y)
                r = 2 * x + y
                result[pl.ds(r, 16, stride=16), :] = value
                mixed[rows, 128 * r : 128 * (r + 1)] = value.astype(bf16)
        filt_ref[stored, :] = result[...].astype(bf16)

    swaps, owns, near, far = {}, {}, {}, {}
    cores, ys, zs = {}, {}, []

    def step_filter(k):
        s0, n = CHUNKS[k]
        if k == 0:
            for copy in pots:
                copy.wait_recv()
        for i in range(8):
            halos[k, i].wait_recv()

        def sub(i, carry):
            filter_rows(s0 // 16 + i)
            return carry

        lax.fori_loop(0, n // 16, sub, 0)
        rows = pl.ds(s0, n)
        swaps[k] = start(
            remote(
                mixed.at[rows, theirs], fb.at[w, rows], swap_ss.at[k], swap_rs.at[k], (gx, gy, w_across)
            )
        )
        for d, to in enumerate(w_near):
            near[k, 0, d] = start(
                remote(
                    mixed.at[rows, mine],
                    fb.at[w, rows],
                    near_ss.at[k, 0, d],
                    near_rs.at[k, 0, d],
                    (gx, gy, to),
                )
            )
        owns[k] = pltpu.make_async_copy(mixed.at[rows, mine], fb.at[w, rows], own_sem.at[k])
        owns[k].start()

    def step_swap(k):
        s0, n = CHUNKS[k]
        rows = pl.ds(s0, n)
        swaps[k].wait_recv()
        for d, to in enumerate(w_near):
            near[k, 1, d] = start(
                remote(
                    fb.at[w_across, rows],
                    fb.at[w_across, rows],
                    near_ss.at[k, 1, d],
                    near_rs.at[k, 1, d],
                    (gx, gy, to),
                )
            )

    def step_forward(k, t):
        s0, n = CHUNKS[k]
        rows = pl.ds(s0, n)
        for d, origin in enumerate(w_near if t == 0 else w_near_across):
            to = w_near[1 - d]
            near[k, t, d].wait_recv()
            piece = fb.at[origin, rows, pl.ds(512 * d, 512)]
            far[k, t, d] = start(
                remote(piece, piece, far_ss.at[k, t, d], far_rs.at[k, t, d], (gx, gy, to))
            )

    def step_matmul(k):
        s0, n = CHUNKS[k]
        rows = pl.ds(s0, n)
        if k == 0:
            pan_own = pltpu.make_async_copy(lines_of.at[:, mine], pan.at[half], pan_sem.at[0])
            pan_own.start()
            pan_own.wait()
            for copy in panel_swaps:
                copy.wait_recv()
        owns[k].wait()
        for t in range(2):
            for d in range(2):
                far[k, t, d].wait_recv()
        for side, dst in ((core_other, core_send), (core, core_own)):
            lhs = jnp.concatenate(
                [fb[4 * (q // 2) + 2 * side + q % 2, rows, :] for q in range(4)], axis=0
            )
            for rb in range(2):
                out = lax.dot_general(lhs, pan[rb], NT, preferred_element_type=f32) * scale
                for q in range(4):
                    dst[q // 2, q % 2, rb, rows, :] = out[n * q : n * (q + 1)]
            if dst is core_send:
                cores[k] = start(
                    remote(
                        core_send.at[:, :, :, rows],
                        core_recv.at[:, :, :, rows],
                        core_ss.at[k],
                        core_rs.at[k],
                        (gx_core, gy, w),
                    )
                )

    y_plan = (
        (ylo_other, half, (gx_ylo, gy, w)),
        (ylo, half_other, (gx, gy, w_across)),
        (ylo_other, half_other, (gx_ylo, gy, w_across)),
    )

    def step_core(k):
        s0, n = CHUNKS[k]
        rows = pl.ds(s0, n)
        cores[k].wait_recv()
        for j, (yl, yh, device) in enumerate(y_plan):
            for q in range(2):
                value = core_own[yl, q, yh, rows, :] + core_recv[yl, q, yh, rows, :]
                y_send[j, q, rows, :] = value.astype(bf16)
            ys[k, j] = start(
                remote(
                    y_send.at[j, :, rows], y_recv.at[j, :, rows], y_ss.at[k, j], y_rs.at[k, j], device
                )
            )
        for q in range(2):
            total[q, rows, :] = core_own[ylo, q, half, rows, :] + core_recv[ylo, q, half, rows, :]

    def step_y(k):
        s0, n = CHUNKS[k]
        rows = pl.ds(s0, n)
        for j in range(3):
            ys[k, j].wait_recv()
        for q in range(2):
            value = total[q, rows, :]
            for j in range(3):
                value = value + y_recv[j, q, rows, :].astype(f32)
            total[q, rows, :] = value
        done_before = s0 // 36
        for c in range(done_before, (s0 + n) // 36):
            for q in range(2):
                block = total[q, 36 * c : 36 * (c + 1), :]
                target = 4 * q + c

                @pl.when(target == gy)
                def _():
                    summed[0:36, :] = block

                @pl.when(target != gy)
                def _():
                    z_send[target, 0:36, :] = block.astype(bf16)
                    remote(
                        z_send.at[target], z_recv.at[gy], z_ss.at[target], z_rs.at[gy], (gx, target, w)
                    ).start()

    last = len(CHUNKS) - 1
    for k in range(last + 1):
        step_filter(k)
        if k < last:
            send_edges(k + 1)
        swap_panels((2, 2, 0)[k])
        if k > 0:
            step_forward(k - 1, 1)
        step_swap(k)
        if k < last:
            step_forward(k, 0)
    step_matmul(0)
    step_forward(last, 0)
    step_core(0)
    step_matmul(1)
    step_forward(last, 1)
    step_core(1)
    step_matmul(last)
    step_y(0)
    step_core(last)
    step_y(1)
    step_y(last)

    for s in range(8):

        @pl.when(s != gy)
        def _():
            copy = remote(z_send.at[s], z_recv.at[s], z_ss.at[s], z_rs.at[s], (gx, s, w))
            copy.wait_recv()
            summed[0:36, :] += z_recv[s, 0:36, :].astype(f32)
            copy.wait_send()

    lanes = out_ref.shape[2]
    for p in range(2):
        out_ref[:, p, :] = summed[0:36, lanes * p : lanes * (p + 1)]
    for copy in pending:
        copy.wait_send()


def body(orbitals, potential, panels):
    bands, lx, ly, lz = orbitals.shape
    cells = lx * ly * lz
    panel_count = panels.shape[0]
    lines = panel_count * bands
    scale = 1.0 / math.sqrt(cells * lax.axis_size("gx") * lax.axis_size("gy"))
    bf16, f32 = jnp.bfloat16, jnp.float32
    c = len(CHUNKS)
    dma = pltpu.SemaphoreType.DMA
    filtered, sums = pl.pallas_call(
        functools.partial(kernel, scale),
        out_shape=(
            jax.ShapeDtypeStruct((bands * lx * ly, lz), bf16),
            jax.ShapeDtypeStruct((36, panel_count, bands), f32),
        ),
        in_specs=[pl.BlockSpec(memory_space=pltpu.VMEM)] * 3,
        out_specs=(pl.BlockSpec(memory_space=pltpu.VMEM),) * 2,
        scratch_shapes=[
            pltpu.VMEM((4, lx * ly, lz), f32),
            pltpu.VMEM((2, bands * lx * ly, lz), bf16),
            pltpu.VMEM((2, bands, 512), bf16),
            pltpu.VMEM((4, bands, 128), bf16),
            pltpu.VMEM((2, lines, cells // 2), bf16),
            pltpu.VMEM((bands, 1024), bf16),
            pltpu.VMEM((lines, cells), bf16),
            pltpu.VMEM((256, lz), f32),
            pltpu.VMEM((2, 256, lz), f32),
            pltpu.VMEM((256, lz), f32),
            pltpu.VMEM((36, 16, 128), f32),
            pltpu.VMEM((bands, cells), bf16),
            pltpu.VMEM((8, bands, cells // 2), bf16),
            pltpu.VMEM((2, 2, 2, bands, lines), f32),
            pltpu.VMEM((2, 2, 2, bands, lines), f32),
            pltpu.VMEM((2, 2, 2, bands, lines), f32),
            pltpu.VMEM((3, 2, bands, lines), bf16),
            pltpu.VMEM((3, 2, bands, lines), bf16),
            pltpu.VMEM((2, bands, lines), f32),
            pltpu.VMEM((40, lines), f32),
            pltpu.VMEM((8, 48, lines), bf16),
            pltpu.VMEM((8, 48, lines), bf16),
            dma((c, 8)),
            dma((c, 8)),
            dma((4,)),
            dma((4,)),
            dma((1,)),
            dma((6,)),
            dma((6,)),
            dma((c,)),
            dma((c,)),
            dma((c,)),
            dma((c, 2, 2)),
            dma((c, 2, 2)),
            dma((c, 2, 2)),
            dma((c, 2, 2)),
            dma((c,)),
            dma((c,)),
            dma((c, 3)),
            dma((c, 3)),
            dma((8,)),
            dma((8,)),
        ],
        compiler_params=pltpu.CompilerParams(
            collective_id=0, has_side_effects=True, vmem_limit_bytes=48 << 20
        ),
        cost_estimate=pl.CostEstimate(
            flops=2 * lines * bands * 8 * cells, bytes_accessed=4 << 20, transcendentals=0
        ),
    )(
        orbitals.reshape(bands * lx * ly, lz),
        potential.reshape(lx * ly, lz),
        panels.reshape(lines * lx * ly, lz),
    )
    margin = sums.transpose(1, 2, 0)
    return filtered.reshape(orbitals.shape), margin


def solution(mesh):
    return jax.shard_map(
        body,
        mesh=mesh,
        in_specs=(
            P("band", "gx", "gy", None),
            P("gx", "gy", None),
            P(None, "band", "gx", "gy", None),
        ),
        out_specs=(P("band", "gx", "gy", None), P(None, "band", ("gx", "gy"))),
        check_vma=False,
    )
```

```python
import functools
import math

import jax
import jax.numpy as jnp
from jax import lax
from jax.experimental import pallas as pl
from jax.experimental.pallas import tpu as pltpu
from jax.sharding import PartitionSpec as P

MESH = pl.DeviceIdType.MESH
NT = (((1,), (1,)), ((), ()))
CHUNKS = ((0, 48), (48, 64), (112, 32))
PIECE = 48


def kernel(
    scale,
    o_hbm,
    pot_hbm,
    p_hbm,
    filt_ref,
    out_ref,
    o_ref,
    pot_ref,
    p_ref,
    load_sem,
    potn,
    yb,
    xb,
    db,
    pan,
    edge,
    lines_of,
    raw,
    side,
    result,
    first,
    mixed,
    fb,
    core_send,
    core_own,
    core_recv,
    y_send,
    y_recv,
    total,
    summed,
    z_send,
    z_recv,
    halo_ss,
    halo_rs,
    pot_ss,
    pot_rs,
    pan_sem,
    pan_ss,
    pan_rs,
    own_sem,
    swap_ss,
    swap_rs,
    near_ss,
    near_rs,
    far_ss,
    far_rs,
    core_ss,
    core_rs,
    y_ss,
    y_rs,
    z_ss,
    z_rs,
):
    bf16, f32 = jnp.bfloat16, jnp.float32
    gx, gy, w = lax.axis_index("gx"), lax.axis_index("gy"), lax.axis_index("band")
    ylo, core = gx // 2, gx % 2
    yhi, xx = w // 4, w % 4
    ylo_other, core_other = 1 - ylo, 1 - core
    half = (xx // 2 + xx) % 2
    half_other = 1 - half
    gx_prev, gx_next = (gx + 3) % 4, (gx + 1) % 4
    gy_prev, gy_next = (gy + 7) % 8, (gy + 1) % 8
    xx_across = xx + 1 - 2 * (xx % 2)
    w_across = yhi * 4 + xx_across
    w_near = ((1 - yhi) * 4 + xx, yhi * 4 + 3 - xx)
    w_near_across = ((1 - yhi) * 4 + xx_across, yhi * 4 + 3 - xx_across)
    gx_core, gx_ylo = ylo * 2 + core_other, ylo_other * 2 + core

    loads = [
        pltpu.make_async_copy(src, dst, load_sem.at[i])
        for i, (src, dst) in enumerate(((o_hbm, o_ref), (pot_hbm, pot_ref), (p_hbm, p_ref)))
    ]
    for copy in loads:
        copy.start()
    barrier = pltpu.get_barrier_semaphore()
    partners = [(gx_prev, gy, w), (gx_next, gy, w)]
    partners += [(gx, (gy + d) % 8, w) for d in range(1, 8)]
    partners += [(a, b, w) for a in (gx_prev, gx_next) for b in (gy_prev, gy_next)]
    partners += [(gx, gy, w_across), (gx, gy, w_near[0]), (gx, gy, w_near[1])]
    partners += [(gx_ylo, gy, w), (gx_ylo, gy, w_across)]
    for device in partners:
        pl.semaphore_signal(barrier, 1, device_id=device, device_id_type=MESH)

    def spread(src, dst, cell_rows, first_group, groups):
        def group(i, carry):
            raw[...] = src[pl.ds(pl.multiple_of(i * 256, 256), 256), :].astype(f32)
            rows = pl.ds(pl.multiple_of(i * 16, 16), 16)
            for j, r in enumerate(cell_rows):
                dst[rows, 128 * j : 128 * (j + 1)] = raw[pl.ds(r, 16, stride=16), :].astype(bf16)
            return carry

        lax.fori_loop(first_group, first_group + groups, group, 0)

    loads[0].wait()
    spread(o_ref, edge, (0, 1, 2, 3, 12, 13, 14, 15), 0, o_ref.shape[0] // 256)
    loads[1].wait()
    pl.semaphore_wait(barrier, len(partners))

    def remote(src, dst, ss, rs, device):
        return pltpu.make_async_remote_copy(
            src_ref=src, dst_ref=dst, send_sem=ss, recv_sem=rs, device_id=device, device_id_type=MESH
        )

    pending = []

    def start(copy):
        copy.start()
        pending.append(copy)
        return copy

    pots = [
        start(remote(pot_ref, potn.at[i], pot_ss.at[i], pot_rs.at[i], device))
        for i, device in enumerate(
            ((gx_next, gy, w), (gx_prev, gy, w), (gx, gy_next, w), (gx, gy_prev, w))
        )
    ]
    halos = {}

    def send_halo(k, places, plan):
        for i in places:
            src, dst, device = plan[i]
            halos[k, i] = start(remote(src, dst, halo_ss.at[k, i], halo_rs.at[k, i], device))

    def send_layers(k):
        s0, n = CHUNKS[k]
        rows = pl.ds(16 * s0, 16 * n)
        send_halo(
            k,
            (0, 1),
            (
                (o_hbm.at[rows], yb.at[0, rows], (gx, gy_next, w)),
                (o_hbm.at[rows], yb.at[1, rows], (gx, gy_prev, w)),
            ),
        )

    def send_edges(k):
        s0, n = CHUNKS[k]
        rows = pl.ds(s0, n)
        send_halo(
            k,
            range(2, 8),
            (
                None,
                None,
                (edge.at[rows, pl.ds(512, 512)], xb.at[0, rows], (gx_next, gy, w)),
                (edge.at[rows, pl.ds(0, 512)], xb.at[1, rows], (gx_prev, gy, w)),
                (edge.at[rows, pl.ds(896, 128)], db.at[0, rows], (gx_next, gy_next, w)),
                (edge.at[rows, pl.ds(768, 128)], db.at[1, rows], (gx_next, gy_prev, w)),
                (edge.at[rows, pl.ds(128, 128)], db.at[2, rows], (gx_prev, gy_next, w)),
                (edge.at[rows, pl.ds(0, 128)], db.at[3, rows], (gx_prev, gy_prev, w)),
            ),
        )

    send_layers(0)
    send_edges(0)
    for k in range(1, len(CHUNKS)):
        send_layers(k)
    mine, theirs = pl.ds(half * 1024, 1024), pl.ds(half_other * 1024, 1024)
    panel_swaps = []

    def swap_panels(count):
        for _ in range(count):
            i = len(panel_swaps)
            lines = pl.ds(i * PIECE, PIECE)
            spread(p_ref, lines_of, range(16), i * (PIECE // 16), PIECE // 16)
            panel_swaps.append(
                start(
                    remote(
                        lines_of.at[lines, theirs],
                        pan.at[half, lines],
                        pan_ss.at[i],
                        pan_rs.at[i],
                        (gx, gy, w_across),
                    )
                )
            )

    loads[2].wait()
    swap_panels(2)
    z_send[:, 32:48, :] = jnp.zeros((8, 16, z_send.shape[2]), bf16)

    def filter_rows(i):
        rows = pl.ds(pl.multiple_of(i * 16, 16), 16)
        stored = pl.ds(pl.multiple_of(i * 256, 256), 256)
        raw[...] = o_ref[stored, :].astype(f32)
        for d in range(2):
            side[d] = yb[d, stored, :].astype(f32)

        def orb(x, y):
            if 0 <= x < 8:
                if y < 0:
                    return side[0, pl.ds(2 * x + y + 2, 16, stride=16), :]
                if y > 1:
                    return side[1, pl.ds(2 * x + y - 2, 16, stride=16), :]
                return raw[pl.ds(2 * x + y, 16, stride=16), :]
            if 0 <= y < 2:
                d, r = (0, 2 * (x + 2) + y) if x < 0 else (1, 2 * (x - 8) + y)
                piece = xb[d, rows, 128 * r : 128 * (r + 1)]
            else:
                piece = db[(0 if x < 0 else 2) + (0 if y < 0 else 1), rows, :]
            return piece.astype(f32)

        def slot(x, y):
            if 0 <= x < 8:
                return 2 * x + y if 0 <= y < 2 else (16 + x if y < 0 else 24 + x)
            return 32 + y if x < 0 else 34 + y

        def coefficient(x, y):
            if 0 <= x < 8 and 0 <= y < 2:
                p = pot_ref[2 * x + y : 2 * x + y + 1, :]
            elif y < 0:
                p = potn[2, 2 * x + 1 : 2 * x + 2, :]
            elif y > 1:
                p = potn[3, 2 * x : 2 * x + 1, :]
            elif x < 0:
                p = potn[0, 14 + y : 15 + y, :]
            else:
                p = potn[1, y : y + 1, :]
            return (p - 1.0) * (1.0 / 12.0)

        def both(v):
            return pltpu.roll(v, 1, 1) + pltpu.roll(v, 127, 1)

        cells = [(x, y) for x in range(8) for y in range(-1, 3)]
        cells += [(x, y) for x in (-1, 8) for y in (0, 1)]
        for x, y in cells:
            v = orb(x, y)
            s = orb(x + 1, y) + orb(x - 1, y) + orb(x, y + 1) + orb(x, y - 1) + both(v)
            first[slot(x, y)] = (coefficient(x, y) * v - s * (1.0 / 6.0)).astype(bf16).astype(f32)
        for x in range(8):
            for y in range(2):
                v = first[slot(x, y)]
                s = first[slot(x + 1, y)] + first[slot(x - 1, y)] + both(v)
                s = s + first[slot(x, y + 1)] + first[slot(x, y - 1)]
                value = 2.0 * coefficient(x, y) * v - s * (1.0 / 3.0) - orb(x, y)
                r = 2 * x + y
                result[pl.ds(r, 16, stride=16), :] = value
                mixed[rows, 128 * r : 128 * (r + 1)] = value.astype(bf16)
        filt_ref[stored, :] = result[...].astype(bf16)

    swaps, owns, near, far = {}, {}, {}, {}
    cores, ys, zs = {}, {}, []

    def step_filter(k):
        s0, n = CHUNKS[k]
        if k == 0:
            for copy in pots:
                copy.wait_recv()
        for i in range(8):
            halos[k, i].wait_recv()

        def sub(i, carry):
            filter_rows(s0 // 16 + i)
            return carry

        lax.fori_loop(0, n // 16, sub, 0)
        rows = pl.ds(s0, n)
        swaps[k] = start(
            remote(
                mixed.at[rows, theirs], fb.at[w, rows], swap_ss.at[k], swap_rs.at[k], (gx, gy, w_across)
            )
        )
        for d, to in enumerate(w_near):
            near[k, 0, d] = start(
                remote(
                    mixed.at[rows, mine],
                    fb.at[w, rows],
                    near_ss.at[k, 0, d],
                    near_rs.at[k, 0, d],
                    (gx, gy, to),
                )
            )
        owns[k] = pltpu.make_async_copy(mixed.at[rows, mine], fb.at[w, rows], own_sem.at[k])
        owns[k].start()

    def step_swap(k):
        s0, n = CHUNKS[k]
        rows = pl.ds(s0, n)
        swaps[k].wait_recv()
        for d, to in enumerate(w_near):
            near[k, 1, d] = start(
                remote(
                    fb.at[w_across, rows],
                    fb.at[w_across, rows],
                    near_ss.at[k, 1, d],
                    near_rs.at[k, 1, d],
                    (gx, gy, to),
                )
            )

    def step_forward(k, t):
        s0, n = CHUNKS[k]
        rows = pl.ds(s0, n)
        for d, origin in enumerate(w_near if t == 0 else w_near_across):
            to = w_near[1 - d]
            near[k, t, d].wait_recv()
            piece = fb.at[origin, rows, pl.ds(512 * d, 512)]
            far[k, t, d] = start(
                remote(piece, piece, far_ss.at[k, t, d], far_rs.at[k, t, d], (gx, gy, to))
            )

    def step_matmul(k):
        s0, n = CHUNKS[k]
        rows = pl.ds(s0, n)
        if k == 0:
            pan_own = pltpu.make_async_copy(lines_of.at[:, mine], pan.at[half], pan_sem.at[0])
            pan_own.start()
            pan_own.wait()
            for copy in panel_swaps:
                copy.wait_recv()
        owns[k].wait()
        for t in range(2):
            for d in range(2):
                far[k, t, d].wait_recv()
        for side, dst in ((core_other, core_send), (core, core_own)):
            lhs = jnp.concatenate(
                [fb[4 * (q // 2) + 2 * side + q % 2, rows, :] for q in range(4)], axis=0
            )
            for rb in range(2):
                out = lax.dot_general(lhs, pan[rb], NT, preferred_element_type=f32) * scale
                for q in range(4):
                    dst[q // 2, q % 2, rb, rows, :] = out[n * q : n * (q + 1)]
            if dst is core_send:
                cores[k] = start(
                    remote(
                        core_send.at[:, :, :, rows],
                        core_recv.at[:, :, :, rows],
                        core_ss.at[k],
                        core_rs.at[k],
                        (gx_core, gy, w),
                    )
                )

    y_plan = (
        (ylo_other, half, (gx_ylo, gy, w)),
        (ylo, half_other, (gx, gy, w_across)),
        (ylo_other, half_other, (gx_ylo, gy, w_across)),
    )

    def step_core(k):
        s0, n = CHUNKS[k]
        rows = pl.ds(s0, n)
        cores[k].wait_recv()
        for j, (yl, yh, device) in enumerate(y_plan):
            for q in range(2):
                value = core_own[yl, q, yh, rows, :] + core_recv[yl, q, yh, rows, :]
                y_send[j, q, rows, :] = value.astype(bf16)
            ys[k, j] = start(
                remote(
                    y_send.at[j, :, rows], y_recv.at[j, :, rows], y_ss.at[k, j], y_rs.at[k, j], device
                )
            )
        for q in range(2):
            total[q, rows, :] = core_own[ylo, q, half, rows, :] + core_recv[ylo, q, half, rows, :]

    def step_y(k):
        s0, n = CHUNKS[k]
        rows = pl.ds(s0, n)
        for j in range(3):
            ys[k, j].wait_recv()
        for q in range(2):
            value = total[q, rows, :]
            for j in range(3):
                value = value + y_recv[j, q, rows, :].astype(f32)
            total[q, rows, :] = value
        done_before = s0 // 36
        for c in range(done_before, (s0 + n) // 36):
            for q in range(2):
                block = total[q, 36 * c : 36 * (c + 1), :]
                target = 4 * q + c

                @pl.when(target == gy)
                def _():
                    summed[0:36, :] = block

                @pl.when(target != gy)
                def _():
                    z_send[target, 0:36, :] = block.astype(bf16)
                    remote(
                        z_send.at[target], z_recv.at[gy], z_ss.at[target], z_rs.at[gy], (gx, target, w)
                    ).start()

    last = len(CHUNKS) - 1
    for k in range(last + 1):
        step_filter(k)
        if k < last:
            send_edges(k + 1)
        swap_panels((2, 2, 0)[k])
        if k > 0:
            step_forward(k - 1, 1)
        step_swap(k)
        if k < last:
            step_forward(k, 0)
    step_matmul(0)
    step_forward(last, 0)
    step_core(0)
    step_matmul(1)
    step_forward(last, 1)
    step_core(1)
    step_matmul(last)
    step_y(0)
    step_core(last)
    step_y(1)
    step_y(last)

    for s in range(8):

        @pl.when(s != gy)
        def _():
            copy = remote(z_send.at[s], z_recv.at[s], z_ss.at[s], z_rs.at[s], (gx, s, w))
            copy.wait_recv()
            summed[0:36, :] += z_recv[s, 0:36, :].astype(f32)
            copy.wait_send()

    lanes = out_ref.shape[2]
    for p in range(2):
        out_ref[:, p, :] = summed[0:36, lanes * p : lanes * (p + 1)]
    for copy in pending:
        copy.wait_send()


def body(orbitals, potential, panels):
    bands, lx, ly, lz = orbitals.shape
    cells = lx * ly * lz
    panel_count = panels.shape[0]
    lines = panel_count * bands
    scale = 1.0 / math.sqrt(cells * lax.axis_size("gx") * lax.axis_size("gy"))
    bf16, f32 = jnp.bfloat16, jnp.float32
    c = len(CHUNKS)
    dma = pltpu.SemaphoreType.DMA
    filtered, sums = pl.pallas_call(
        functools.partial(kernel, scale),
        out_shape=(
            jax.ShapeDtypeStruct((bands * lx * ly, lz), bf16),
            jax.ShapeDtypeStruct((36, panel_count, bands), f32),
        ),
        in_specs=[pl.BlockSpec(memory_space=pltpu.HBM)] * 3,
        out_specs=(pl.BlockSpec(memory_space=pltpu.VMEM),) * 2,
        scratch_shapes=[
            pltpu.VMEM((bands * lx * ly, lz), bf16),
            pltpu.VMEM((lx * ly, lz), f32),
            pltpu.VMEM((lines * lx * ly, lz), bf16),
            dma((3,)),
            pltpu.VMEM((4, lx * ly, lz), f32),
            pltpu.VMEM((2, bands * lx * ly, lz), bf16),
            pltpu.VMEM((2, bands, 512), bf16),
            pltpu.VMEM((4, bands, 128), bf16),
            pltpu.VMEM((2, lines, cells // 2), bf16),
            pltpu.VMEM((bands, 1024), bf16),
            pltpu.VMEM((lines, cells), bf16),
            pltpu.VMEM((256, lz), f32),
            pltpu.VMEM((2, 256, lz), f32),
            pltpu.VMEM((256, lz), f32),
            pltpu.VMEM((36, 16, 128), f32),
            pltpu.VMEM((bands, cells), bf16),
            pltpu.VMEM((8, bands, cells // 2), bf16),
            pltpu.VMEM((2, 2, 2, bands, lines), f32),
            pltpu.VMEM((2, 2, 2, bands, lines), f32),
            pltpu.VMEM((2, 2, 2, bands, lines), f32),
            pltpu.VMEM((3, 2, bands, lines), bf16),
            pltpu.VMEM((3, 2, bands, lines), bf16),
            pltpu.VMEM((2, bands, lines), f32),
            pltpu.VMEM((40, lines), f32),
            pltpu.VMEM((8, 48, lines), bf16),
            pltpu.VMEM((8, 48, lines), bf16),
            dma((c, 8)),
            dma((c, 8)),
            dma((4,)),
            dma((4,)),
            dma((1,)),
            dma((6,)),
            dma((6,)),
            dma((c,)),
            dma((c,)),
            dma((c,)),
            dma((c, 2, 2)),
            dma((c, 2, 2)),
            dma((c, 2, 2)),
            dma((c, 2, 2)),
            dma((c,)),
            dma((c,)),
            dma((c, 3)),
            dma((c, 3)),
            dma((8,)),
            dma((8,)),
        ],
        compiler_params=pltpu.CompilerParams(
            collective_id=0, has_side_effects=True, vmem_limit_bytes=62 << 20
        ),
        cost_estimate=pl.CostEstimate(
            flops=2 * lines * bands * 8 * cells, bytes_accessed=4 << 20, transcendentals=0
        ),
    )(
        orbitals.reshape(bands * lx * ly, lz),
        potential.reshape(lx * ly, lz),
        panels.reshape(lines * lx * ly, lz),
    )
    margin = sums.transpose(1, 2, 0)
    return filtered.reshape(orbitals.shape), margin


def solution(mesh):
    return jax.shard_map(
        body,
        mesh=mesh,
        in_specs=(
            P("band", "gx", "gy", None),
            P("gx", "gy", None),
            P(None, "band", "gx", "gy", None),
        ),
        out_specs=(P("band", "gx", "gy", None), P(None, "band", ("gx", "gy"))),
        check_vma=False,
    )
```

```python
import functools
import math

import jax
import jax.numpy as jnp
from jax import lax
from jax.experimental import pallas as pl
from jax.experimental.pallas import tpu as pltpu
from jax.sharding import PartitionSpec as P

MESH = pl.DeviceIdType.MESH
NT = (((1,), (1,)), ((), ()))
CHUNKS = ((0, 48), (48, 64), (112, 32))
PIECE = 48


def kernel(
    scale,
    o_hbm,
    pot_hbm,
    p_hbm,
    filt_ref,
    out_ref,
    o_ref,
    pot_ref,
    p_ref,
    load_sem,
    potn,
    yb,
    xb,
    db,
    pan,
    edge,
    lines_of,
    raw,
    side,
    result,
    first,
    mixed,
    fb,
    core_send,
    core_own,
    core_recv,
    y_send,
    y_recv,
    total,
    summed,
    z_send,
    z_recv,
    halo_ss,
    halo_rs,
    pot_ss,
    pot_rs,
    pan_sem,
    pan_ss,
    pan_rs,
    own_sem,
    swap_ss,
    swap_rs,
    near_ss,
    near_rs,
    far_ss,
    far_rs,
    core_ss,
    core_rs,
    y_ss,
    y_rs,
    z_ss,
    z_rs,
):
    bf16, f32 = jnp.bfloat16, jnp.float32
    gx, gy, w = lax.axis_index("gx"), lax.axis_index("gy"), lax.axis_index("band")
    ylo, core = gx // 2, gx % 2
    yhi, xx = w // 4, w % 4
    ylo_other, core_other = 1 - ylo, 1 - core
    half = (xx // 2 + xx) % 2
    half_other = 1 - half
    gx_prev, gx_next = (gx + 3) % 4, (gx + 1) % 4
    gy_prev, gy_next = (gy + 7) % 8, (gy + 1) % 8
    xx_across = xx + 1 - 2 * (xx % 2)
    w_across = yhi * 4 + xx_across
    w_near = ((1 - yhi) * 4 + xx, yhi * 4 + 3 - xx)
    w_near_across = ((1 - yhi) * 4 + xx_across, yhi * 4 + 3 - xx_across)
    gx_core, gx_ylo = ylo * 2 + core_other, ylo_other * 2 + core

    loads = [
        pltpu.make_async_copy(src, dst, load_sem.at[i])
        for i, (src, dst) in enumerate(((o_hbm, o_ref), (pot_hbm, pot_ref), (p_hbm, p_ref)))
    ]
    for copy in loads:
        copy.start()
    barrier = pltpu.get_barrier_semaphore()
    partners = [(gx_prev, gy, w), (gx_next, gy, w)]
    partners += [(gx, (gy + d) % 8, w) for d in range(1, 8)]
    partners += [(a, b, w) for a in (gx_prev, gx_next) for b in (gy_prev, gy_next)]
    partners += [(gx, gy, w_across), (gx, gy, w_near[0]), (gx, gy, w_near[1])]
    partners += [(gx_ylo, gy, w), (gx_ylo, gy, w_across)]
    for device in partners:
        pl.semaphore_signal(barrier, 1, device_id=device, device_id_type=MESH)

    def spread(src, dst, cell_rows, first_group, groups):
        def group(i, carry):
            raw[...] = src[pl.ds(pl.multiple_of(i * 256, 256), 256), :].astype(f32)
            rows = pl.ds(pl.multiple_of(i * 16, 16), 16)
            for j, r in enumerate(cell_rows):
                dst[rows, 128 * j : 128 * (j + 1)] = raw[pl.ds(r, 16, stride=16), :].astype(bf16)
            return carry

        lax.fori_loop(first_group, first_group + groups, group, 0)

    loads[0].wait()
    spread(o_ref, edge, (0, 1, 2, 3, 12, 13, 14, 15), 0, o_ref.shape[0] // 256)
    loads[1].wait()
    pl.semaphore_wait(barrier, len(partners))

    def remote(src, dst, ss, rs, device):
        return pltpu.make_async_remote_copy(
            src_ref=src, dst_ref=dst, send_sem=ss, recv_sem=rs, device_id=device, device_id_type=MESH
        )

    pending = []

    def start(copy):
        copy.start()
        pending.append(copy)
        return copy

    pots = [
        start(remote(pot_ref, potn.at[i], pot_ss.at[i], pot_rs.at[i], device))
        for i, device in enumerate(
            ((gx_next, gy, w), (gx_prev, gy, w), (gx, gy_next, w), (gx, gy_prev, w))
        )
    ]
    halos = {}

    def send_halo(k, places, plan):
        for i in places:
            src, dst, device = plan[i]
            halos[k, i] = start(remote(src, dst, halo_ss.at[k, i], halo_rs.at[k, i], device))

    def send_layers(k):
        s0, n = CHUNKS[k]
        rows = pl.ds(16 * s0, 16 * n)
        send_halo(
            k,
            (0, 1),
            (
                (o_hbm.at[rows], yb.at[0, rows], (gx, gy_next, w)),
                (o_hbm.at[rows], yb.at[1, rows], (gx, gy_prev, w)),
            ),
        )

    def send_edges(k):
        s0, n = CHUNKS[k]
        rows = pl.ds(s0, n)
        send_halo(
            k,
            range(2, 8),
            (
                None,
                None,
                (edge.at[rows, pl.ds(512, 512)], xb.at[0, rows], (gx_next, gy, w)),
                (edge.at[rows, pl.ds(0, 512)], xb.at[1, rows], (gx_prev, gy, w)),
                (edge.at[rows, pl.ds(896, 128)], db.at[0, rows], (gx_next, gy_next, w)),
                (edge.at[rows, pl.ds(768, 128)], db.at[1, rows], (gx_next, gy_prev, w)),
                (edge.at[rows, pl.ds(128, 128)], db.at[2, rows], (gx_prev, gy_next, w)),
                (edge.at[rows, pl.ds(0, 128)], db.at[3, rows], (gx_prev, gy_prev, w)),
            ),
        )

    send_layers(0)
    send_edges(0)
    send_layers(1)
    send_edges(1)
    send_layers(2)
    mine, theirs = pl.ds(half * 1024, 1024), pl.ds(half_other * 1024, 1024)
    panel_swaps = []

    def swap_panels(count):
        for _ in range(count):
            i = len(panel_swaps)
            lines = pl.ds(i * PIECE, PIECE)
            spread(p_ref, lines_of, range(16), i * (PIECE // 16), PIECE // 16)
            panel_swaps.append(
                start(
                    remote(
                        lines_of.at[lines, theirs],
                        pan.at[half, lines],
                        pan_ss.at[i],
                        pan_rs.at[i],
                        (gx, gy, w_across),
                    )
                )
            )

    loads[2].wait()
    swap_panels(2)
    z_send[:, 32:48, :] = jnp.zeros((8, 16, z_send.shape[2]), bf16)

    def filter_rows(i):
        rows = pl.ds(pl.multiple_of(i * 16, 16), 16)
        stored = pl.ds(pl.multiple_of(i * 256, 256), 256)
        raw[...] = o_ref[stored, :].astype(f32)
        for d in range(2):
            side[d] = yb[d, stored, :].astype(f32)

        def orb(x, y):
            if 0 <= x < 8:
                if y < 0:
                    return side[0, pl.ds(2 * x + y + 2, 16, stride=16), :]
                if y > 1:
                    return side[1, pl.ds(2 * x + y - 2, 16, stride=16), :]
                return raw[pl.ds(2 * x + y, 16, stride=16), :]
            if 0 <= y < 2:
                d, r = (0, 2 * (x + 2) + y) if x < 0 else (1, 2 * (x - 8) + y)
                piece = xb[d, rows, 128 * r : 128 * (r + 1)]
            else:
                piece = db[(0 if x < 0 else 2) + (0 if y < 0 else 1), rows, :]
            return piece.astype(f32)

        def slot(x, y):
            if 0 <= x < 8:
                return 2 * x + y if 0 <= y < 2 else (16 + x if y < 0 else 24 + x)
            return 32 + y if x < 0 else 34 + y

        def coefficient(x, y):
            if 0 <= x < 8 and 0 <= y < 2:
                p = pot_ref[2 * x + y : 2 * x + y + 1, :]
            elif y < 0:
                p = potn[2, 2 * x + 1 : 2 * x + 2, :]
            elif y > 1:
                p = potn[3, 2 * x : 2 * x + 1, :]
            elif x < 0:
                p = potn[0, 14 + y : 15 + y, :]
            else:
                p = potn[1, y : y + 1, :]
            return (p - 1.0) * (1.0 / 12.0)

        def both(v):
            return pltpu.roll(v, 1, 1) + pltpu.roll(v, 127, 1)

        cells = [(x, y) for x in range(8) for y in range(-1, 3)]
        cells += [(x, y) for x in (-1, 8) for y in (0, 1)]
        for x, y in cells:
            v = orb(x, y)
            s = orb(x + 1, y) + orb(x - 1, y) + orb(x, y + 1) + orb(x, y - 1) + both(v)
            first[slot(x, y)] = (coefficient(x, y) * v - s * (1.0 / 6.0)).astype(bf16).astype(f32)
        for x in range(8):
            for y in range(2):
                v = first[slot(x, y)]
                s = first[slot(x + 1, y)] + first[slot(x - 1, y)] + both(v)
                s = s + first[slot(x, y + 1)] + first[slot(x, y - 1)]
                value = 2.0 * coefficient(x, y) * v - s * (1.0 / 3.0) - orb(x, y)
                r = 2 * x + y
                result[pl.ds(r, 16, stride=16), :] = value
                mixed[rows, 128 * r : 128 * (r + 1)] = value.astype(bf16)
        filt_ref[stored, :] = result[...].astype(bf16)

    swaps, owns, near, far = {}, {}, {}, {}
    cores, ys, zs = {}, {}, []

    def step_filter(k):
        s0, n = CHUNKS[k]
        if k == 0:
            for copy in pots:
                copy.wait_recv()
        for i in range(8):
            halos[k, i].wait_recv()

        def sub(i, carry):
            filter_rows(s0 // 16 + i)
            return carry

        lax.fori_loop(0, n // 16, sub, 0)
        rows = pl.ds(s0, n)
        swaps[k] = start(
            remote(
                mixed.at[rows, theirs], fb.at[w, rows], swap_ss.at[k], swap_rs.at[k], (gx, gy, w_across)
            )
        )
        for d, to in enumerate(w_near):
            near[k, 0, d] = start(
                remote(
                    mixed.at[rows, mine],
                    fb.at[w, rows],
                    near_ss.at[k, 0, d],
                    near_rs.at[k, 0, d],
                    (gx, gy, to),
                )
            )
        owns[k] = pltpu.make_async_copy(mixed.at[rows, mine], fb.at[w, rows], own_sem.at[k])
        owns[k].start()

    def step_swap(k):
        s0, n = CHUNKS[k]
        rows = pl.ds(s0, n)
        swaps[k].wait_recv()
        for d, to in enumerate(w_near):
            near[k, 1, d] = start(
                remote(
                    fb.at[w_across, rows],
                    fb.at[w_across, rows],
                    near_ss.at[k, 1, d],
                    near_rs.at[k, 1, d],
                    (gx, gy, to),
                )
            )

    def step_forward(k, t):
        s0, n = CHUNKS[k]
        rows = pl.ds(s0, n)
        for d, origin in enumerate(w_near if t == 0 else w_near_across):
            to = w_near[1 - d]
            near[k, t, d].wait_recv()
            piece = fb.at[origin, rows, pl.ds(512 * d, 512)]
            far[k, t, d] = start(
                remote(piece, piece, far_ss.at[k, t, d], far_rs.at[k, t, d], (gx, gy, to))
            )

    def step_matmul(k):
        s0, n = CHUNKS[k]
        rows = pl.ds(s0, n)
        if k == 0:
            pan_own = pltpu.make_async_copy(lines_of.at[:, mine], pan.at[half], pan_sem.at[0])
            pan_own.start()
            pan_own.wait()
            for copy in panel_swaps:
                copy.wait_recv()
        owns[k].wait()
        for t in range(2):
            for d in range(2):
                far[k, t, d].wait_recv()
        for side, dst in ((core_other, core_send), (core, core_own)):
            lhs = jnp.concatenate(
                [fb[4 * (q // 2) + 2 * side + q % 2, rows, :] for q in range(4)], axis=0
            )
            for rb in range(2):
                out = lax.dot_general(lhs, pan[rb], NT, preferred_element_type=f32) * scale
                for q in range(4):
                    dst[q // 2, q % 2, rb, rows, :] = out[n * q : n * (q + 1)]
            if dst is core_send:
                cores[k] = start(
                    remote(
                        core_send.at[:, :, :, rows],
                        core_recv.at[:, :, :, rows],
                        core_ss.at[k],
                        core_rs.at[k],
                        (gx_core, gy, w),
                    )
                )

    y_plan = (
        (ylo_other, half, (gx_ylo, gy, w)),
        (ylo, half_other, (gx, gy, w_across)),
        (ylo_other, half_other, (gx_ylo, gy, w_across)),
    )

    def step_core(k):
        s0, n = CHUNKS[k]
        rows = pl.ds(s0, n)
        cores[k].wait_recv()
        for j, (yl, yh, device) in enumerate(y_plan):
            for q in range(2):
                value = core_own[yl, q, yh, rows, :] + core_recv[yl, q, yh, rows, :]
                y_send[j, q, rows, :] = value.astype(bf16)
            ys[k, j] = start(
                remote(
                    y_send.at[j, :, rows], y_recv.at[j, :, rows], y_ss.at[k, j], y_rs.at[k, j], device
                )
            )
        for q in range(2):
            total[q, rows, :] = core_own[ylo, q, half, rows, :] + core_recv[ylo, q, half, rows, :]

    def step_y(k):
        s0, n = CHUNKS[k]
        rows = pl.ds(s0, n)
        for j in range(3):
            ys[k, j].wait_recv()
        for q in range(2):
            value = total[q, rows, :]
            for j in range(3):
                value = value + y_recv[j, q, rows, :].astype(f32)
            total[q, rows, :] = value
        done_before = s0 // 36
        for c in range(done_before, (s0 + n) // 36):
            for q in range(2):
                block = total[q, 36 * c : 36 * (c + 1), :]
                target = 4 * q + c

                @pl.when(target == gy)
                def _():
                    summed[0:36, :] = block

                @pl.when(target != gy)
                def _():
                    z_send[target, 0:36, :] = block.astype(bf16)
                    remote(
                        z_send.at[target], z_recv.at[gy], z_ss.at[target], z_rs.at[gy], (gx, target, w)
                    ).start()

    last = len(CHUNKS) - 1
    for k in range(last + 1):
        step_filter(k)
        if k == 0:
            send_edges(2)
        swap_panels((2, 2, 0)[k])
        if k > 0:
            step_forward(k - 1, 1)
        step_swap(k)
        if k < last:
            step_forward(k, 0)
    step_matmul(0)
    step_forward(last, 0)
    step_core(0)
    step_matmul(1)
    step_forward(last, 1)
    step_core(1)
    step_matmul(last)
    step_y(0)
    step_core(last)
    step_y(1)
    step_y(last)

    for s in range(8):

        @pl.when(s != gy)
        def _():
            copy = remote(z_send.at[s], z_recv.at[s], z_ss.at[s], z_rs.at[s], (gx, s, w))
            copy.wait_recv()
            summed[0:36, :] += z_recv[s, 0:36, :].astype(f32)
            copy.wait_send()

    lanes = out_ref.shape[2]
    for p in range(2):
        out_ref[:, p, :] = summed[0:36, lanes * p : lanes * (p + 1)]
    for copy in pending:
        copy.wait_send()


def body(orbitals, potential, panels):
    bands, lx, ly, lz = orbitals.shape
    cells = lx * ly * lz
    panel_count = panels.shape[0]
    lines = panel_count * bands
    scale = 1.0 / math.sqrt(cells * lax.axis_size("gx") * lax.axis_size("gy"))
    bf16, f32 = jnp.bfloat16, jnp.float32
    c = len(CHUNKS)
    dma = pltpu.SemaphoreType.DMA
    filtered, sums = pl.pallas_call(
        functools.partial(kernel, scale),
        out_shape=(
            jax.ShapeDtypeStruct((bands * lx * ly, lz), bf16),
            jax.ShapeDtypeStruct((36, panel_count, bands), f32),
        ),
        in_specs=[pl.BlockSpec(memory_space=pltpu.HBM)] * 3,
        out_specs=(pl.BlockSpec(memory_space=pltpu.VMEM),) * 2,
        scratch_shapes=[
            pltpu.VMEM((bands * lx * ly, lz), bf16),
            pltpu.VMEM((lx * ly, lz), f32),
            pltpu.VMEM((lines * lx * ly, lz), bf16),
            dma((3,)),
            pltpu.VMEM((4, lx * ly, lz), f32),
            pltpu.VMEM((2, bands * lx * ly, lz), bf16),
            pltpu.VMEM((2, bands, 512), bf16),
            pltpu.VMEM((4, bands, 128), bf16),
            pltpu.VMEM((2, lines, cells // 2), bf16),
            pltpu.VMEM((bands, 1024), bf16),
            pltpu.VMEM((lines, cells), bf16),
            pltpu.VMEM((256, lz), f32),
            pltpu.VMEM((2, 256, lz), f32),
            pltpu.VMEM((256, lz), f32),
            pltpu.VMEM((36, 16, 128), f32),
            pltpu.VMEM((bands, cells), bf16),
            pltpu.VMEM((8, bands, cells // 2), bf16),
            pltpu.VMEM((2, 2, 2, bands, lines), f32),
            pltpu.VMEM((2, 2, 2, bands, lines), f32),
            pltpu.VMEM((2, 2, 2, bands, lines), f32),
            pltpu.VMEM((3, 2, bands, lines), bf16),
            pltpu.VMEM((3, 2, bands, lines), bf16),
            pltpu.VMEM((2, bands, lines), f32),
            pltpu.VMEM((40, lines), f32),
            pltpu.VMEM((8, 48, lines), bf16),
            pltpu.VMEM((8, 48, lines), bf16),
            dma((c, 8)),
            dma((c, 8)),
            dma((4,)),
            dma((4,)),
            dma((1,)),
            dma((6,)),
            dma((6,)),
            dma((c,)),
            dma((c,)),
            dma((c,)),
            dma((c, 2, 2)),
            dma((c, 2, 2)),
            dma((c, 2, 2)),
            dma((c, 2, 2)),
            dma((c,)),
            dma((c,)),
            dma((c, 3)),
            dma((c, 3)),
            dma((8,)),
            dma((8,)),
        ],
        compiler_params=pltpu.CompilerParams(
            collective_id=0, has_side_effects=True, vmem_limit_bytes=62 << 20
        ),
        cost_estimate=pl.CostEstimate(
            flops=2 * lines * bands * 8 * cells, bytes_accessed=4 << 20, transcendentals=0
        ),
    )(
        orbitals.reshape(bands * lx * ly, lz),
        potential.reshape(lx * ly, lz),
        panels.reshape(lines * lx * ly, lz),
    )
    margin = sums.transpose(1, 2, 0)
    return filtered.reshape(orbitals.shape), margin


def solution(mesh):
    return jax.shard_map(
        body,
        mesh=mesh,
        in_specs=(
            P("band", "gx", "gy", None),
            P("gx", "gy", None),
            P(None, "band", "gx", "gy", None),
        ),
        out_specs=(P("band", "gx", "gy", None), P(None, "band", ("gx", "gy"))),
        check_vma=False,
    )
```
